32 devices in a mesh: parts: 2 (over x), beam: 16 (over z, y, core).
Axes of the slice: x: 2, y: 2, z: 4, core: 2. Of those that a mesh axis runs over, the one named last changes fastest.
Arguments:
- smatrix: bfloat16 [144, 144, 4, 2048], P(None, None, 'parts', 'beam'), parts along dimension 2, may hold values from -6 to 6
- amplitude: float32 [2048], P('beam'), may hold values from 0.5 to 13.5
- aberration: float32 [2048], P('beam'), may hold values from -3.140625 to 3.140625
- beam_list: int32 [2048, 2], P('beam'), may hold values from -64 to 63
- positions: int32 [2, 64, 2], replicated, may hold values from 0 to 127
- anchors: int32 [2, 2], replicated, may hold values from 0 to 16
- masks: int32 [4, 128, 128], replicated, may hold values from 0 to 1, as said below
Outputs:
- signals: float32 [4, 64, 4], P('parts', 'beam'), parts along dimension 0
The draws below stay inside these ranges and needn't reach their ends.
There are 2 independent parts, one for each index of `parts`. The reference program is written for one: setup_inputs(seed, part) draws one part's arguments, and reference() takes and returns one part's arrays. A program takes and returns all parts, laid end to end along the dimension named above; an argument that names none is the same for every part. Nothing has to cross between parts.
Inputs may be any that keep to these rules, and one draw needn't show every extreme that they name: `masks`: each detector's mask is 1 exactly on an annulus of wrapped frequency radii, every annulus holds some frequencies, and every masked frequency has wrapped radius squared below (63) squared.
All inputs are finite; a program needn't handle non-finite values.
Results may differ from the reference program's by a relative error of at most 0.00035.
Values sent between devices are 32-bit elements; how exact they have to be, the bound alone decides.
A program may use at most 128 MiB of HBM per device.

```python
import math
import jax
import jax.numpy as jnp
from jax import lax

BEAMS = 2048
WIN = 128
REG = 144
TILES = 2
PROBES = 64
DET = 4


def draw_amplitude(key, part):
    key = jax.random.fold_in(key, 7)
    base = jax.random.uniform(key, (BEAMS,), jnp.float32, 0.5, 1.5)
    place = jnp.arange(BEAMS, dtype=jnp.float32) / BEAMS
    ramp = 1.0 + 2.0 * place
    return (base * ramp).astype(jnp.float32)


def draw_masks(key, part):
    key = jax.random.fold_in(key, 11)
    inner_key, width_key = jax.random.split(key)
    inner = jax.random.randint(inner_key, (DET,), 0, WIN // 4)
    spread = jax.random.randint(width_key, (DET,), WIN // 16 + 1, WIN // 4 + 1)
    outer = inner + spread
    freq = jnp.arange(WIN, dtype=jnp.int32)
    wrapped = jnp.where(freq < WIN // 2, freq, freq - WIN)
    radius = wrapped[:, None] * wrapped[:, None] + wrapped[None, :] * wrapped[None, :]
    inside = (radius[None] >= (inner * inner)[:, None, None]) & (radius[None] < (outer * outer)[:, None, None])
    return inside.astype(jnp.int32)


def with_ends(result, own_key, least, top_value):
    longest = result.shape.index(max(result.shape))
    spots = []
    for shift in (0, 1):
        where = [jax.random.randint(jax.random.fold_in(own_key, axis), (), 0, length) for axis, length in enumerate(result.shape)]
        where[longest] = (where[longest] + shift) % result.shape[longest]
        spots.append(tuple(where))
    return result.at[spots[0]].set(least).at[spots[1]].set(top_value)


def levels(stream_key, dims, shards, low, largest):
    level = 1.0
    for dim, blocks in shards:
        draws = jax.random.uniform(jax.random.fold_in(jax.random.fold_in(stream_key, 6), dim), (blocks,), jnp.float32, low / len(shards), largest / len(shards))
        level = level * jnp.repeat(jnp.exp(draws), dims[dim] // blocks).reshape((-1,) + (1,) * (len(dims) - 1 - dim))
    return level


def normal_values(stream_key, dims, scale, bound, shards=(), held_as=jnp.bfloat16):
    gain = levels(stream_key, dims, shards, -0.22, 0.18) if shards else 1.0
    drawn = jax.random.normal(stream_key, dims, jnp.float32) * scale * gain
    return jnp.minimum(jnp.maximum(drawn, -bound), bound).astype(held_as)


def setup_inputs(seed: int = 0, part: int = 0) -> dict:
    splits = jax.random.split(jax.random.key(seed), 8)
    own_keys = jax.random.split(jax.random.fold_in(splits[7], part), 8)
    return {
        "smatrix": normal_values(own_keys[0], (REG, REG, 2, BEAMS), 1.0, 6.0, ((3, 16),)),
        "amplitude": draw_amplitude(jax.random.fold_in(splits[7], 71), part),
        "aberration": jnp.clip(jax.random.uniform(splits[2], (BEAMS,), jnp.float32, -3.140625, 3.140625), -3.140625, 3.140625),
        "beam_list": with_ends(jax.random.randint(splits[3], (BEAMS, 2), 0 - WIN // 2, WIN // 2), jax.random.fold_in(splits[3], 1), 0 - WIN // 2, (WIN // 2) - 1).astype(jnp.int32),
        "positions": with_ends(jax.random.randint(splits[4], (TILES, PROBES, 2), 0, WIN), jax.random.fold_in(splits[4], 1), 0, WIN - 1).astype(jnp.int32),
        "anchors": with_ends(jax.random.randint(splits[5], (TILES, 2), 0, REG - WIN + 1), jax.random.fold_in(splits[5], 1), 0, REG - WIN).astype(jnp.int32),
        "masks": draw_masks(jax.random.fold_in(splits[7], 71), part),
    }


def reference(smatrix, amplitude, aberration, beam_list, positions, anchors, masks):
    norm = jnp.sum(amplitude * amplitude)
    mask_table = masks.reshape(DET, WIN * WIN).astype(jnp.float32)
    zero = jnp.zeros((), jnp.int32)
    results = []
    for tile in range(TILES):
        spots = positions[tile]
        phase_index = jnp.remainder(spots[:, 0:1] * beam_list[None, :, 0] + spots[:, 1:2] * beam_list[None, :, 1], WIN)
        theta = aberration[None, :] - (2.0 * math.pi / WIN) * phase_index.astype(jnp.float32)
        coef_re = (amplitude[None, :] * jnp.cos(theta)).astype(jnp.bfloat16)
        coef_im = (amplitude[None, :] * jnp.sin(theta)).astype(jnp.bfloat16)
        corner = anchors[tile].astype(jnp.int32)
        window = lax.dynamic_slice(smatrix, (corner[0], corner[1], zero, zero), (WIN, WIN, 2, BEAMS))
        window = window.reshape(WIN * WIN, 2, BEAMS)
        part_re = window[:, 0, :].T
        part_im = window[:, 1, :].T
        exit_re = jnp.dot(coef_re, part_re, preferred_element_type=jnp.float32) - jnp.dot(coef_im, part_im, preferred_element_type=jnp.float32)
        exit_im = jnp.dot(coef_re, part_im, preferred_element_type=jnp.float32) + jnp.dot(coef_im, part_re, preferred_element_type=jnp.float32)
        wave = lax.complex(exit_re, exit_im).reshape(PROBES, WIN, WIN)
        spectrum = jnp.fft.fft2(wave)
        power = (jnp.real(spectrum) ** 2 + jnp.imag(spectrum) ** 2).reshape(PROBES, WIN * WIN)
        signal = jnp.dot(power, mask_table.T, precision=lax.Precision.HIGHEST) / (norm * WIN * WIN)
        results.append(signal)
    return jnp.stack(results, 0)
```

```python
import functools
import math

import jax
import jax.numpy as jnp
import numpy as np
from jax import lax
from jax.experimental import pallas as pl
from jax.experimental.pallas import tpu as pltpu
from jax.sharding import PartitionSpec as P

TILES = 2
ROUNDS = 8
ROWS = 2
MESH = pl.DeviceIdType.MESH


def coefficients(amplitude, aberration, beam_list, spots, width):
    phase_index = jnp.remainder(
        spots[:, 0:1] * beam_list[None, :, 0] + spots[:, 1:2] * beam_list[None, :, 1], width
    )
    theta = aberration[None, :] - 2.0 * math.pi / width * phase_index.astype(jnp.float32)
    coef_re = (amplitude[None, :] * jnp.cos(theta)).astype(jnp.bfloat16)
    coef_im = (amplitude[None, :] * jnp.sin(theta)).astype(jnp.bfloat16)
    upper = jnp.concatenate([coef_re, -coef_im], 1)
    lower = jnp.concatenate([coef_im, coef_re], 1)
    return jnp.stack([upper, lower], 1)


def window_of(smatrix, corner, width):
    zero = jnp.zeros((), jnp.int32)
    local_beams = smatrix.shape[3]
    window = lax.dynamic_slice(
        smatrix, (corner[0], corner[1], zero, zero), (width, width, 2, local_beams)
    )
    return window.reshape(width * width, 2 * local_beams)


def transform(wave_re, wave_im, width):
    freq = jnp.arange(width, dtype=jnp.int32)
    angle = (
        2.0
        * math.pi
        / width
        * jnp.remainder(freq[:, None] * freq[None, :], width).astype(jnp.float32)
    )
    cosine = jnp.cos(angle)
    sine = jnp.sin(angle)
    high = lax.Precision.HIGHEST
    half_re = jnp.einsum("nrs,sk->nrk", wave_re, cosine, precision=high) + jnp.einsum(
        "nrs,sk->nrk", wave_im, sine, precision=high
    )
    half_im = jnp.einsum("nrs,sk->nrk", wave_im, cosine, precision=high) - jnp.einsum(
        "nrs,sk->nrk", wave_re, sine, precision=high
    )
    full_re = jnp.einsum("jr,nrk->njk", cosine, half_re, precision=high) + jnp.einsum(
        "jr,nrk->njk", sine, half_im, precision=high
    )
    full_im = jnp.einsum("jr,nrk->njk", cosine, half_im, precision=high) - jnp.einsum(
        "jr,nrk->njk", sine, half_re, precision=high
    )
    return (full_re, full_im)


def wave_rows(left, right, count):
    rows = left
    rows = rows.reshape(2 * count, rows.shape[2])
    product = lax.dot_general(
        rows, right, (((1,), (1,)), ((), ())), preferred_element_type=jnp.float32
    )
    product = product.reshape(count, 2, right.shape[0])
    return product


def detect(owned, mask_table, norm, width):
    count = owned.shape[0]
    full_re, full_im = transform(
        owned[:, 0].reshape(count, width, width), owned[:, 1].reshape(count, width, width), width
    )
    power = (full_re * full_re + full_im * full_im).reshape(count, width * width)
    return jnp.einsum("np,dp->nd", power, mask_table, precision=lax.Precision.HIGHEST) / (
        norm * width * width
    )


def local(smatrix, amplitude, aberration, beam_list, positions, anchors, masks):
    width = masks.shape[1]
    detectors = masks.shape[0]
    pixels = width * width
    per_device = positions.shape[1] // lax.axis_size("beam")
    norm = lax.psum(jnp.sum(amplitude * amplitude), "beam")
    mask_table = masks.reshape(detectors, pixels).astype(jnp.float32)
    lefts = []
    rights = []
    for tile in range(TILES):
        lefts.append(coefficients(amplitude, aberration, beam_list, positions[tile], width))
        rights.append(window_of(smatrix, anchors[tile], width))
    outputs = []
    for tile in range(TILES):
        left = lefts[tile]
        right = rights[tile]
        owned = lax.psum_scatter(
            wave_rows(left, right, per_device * lax.axis_size("beam")),
            "beam",
            scatter_dimension=0,
            tiled=True,
        )
        outputs.append(detect(owned, mask_table, norm, width))
    return jnp.stack(outputs, 0)


def fourier(width):
    index = np.arange(width)
    angle = 2.0 * np.pi / width * (np.outer(index, index) % width)
    return np.cos(angle), np.sin(angle)


def halves(table):
    high = table.astype(np.float32).astype(jnp.bfloat16)
    low = (table - high.astype(np.float64)).astype(np.float32).astype(jnp.bfloat16)
    return np.stack([high, low])


def column_table(width):
    cosine, sine = fourier(width)
    table = np.zeros((width, 2, 2, width))
    table[:, 0, 0] = cosine
    table[:, 1, 0] = sine
    table[:, 0, 1] = -sine
    table[:, 1, 1] = cosine
    return halves(table.reshape(2 * width, 2 * width))


def reduce_kernel(
    deep, width, anchors, matrix, coef, fold, power_in, table, out,
    own, from_core, from_y, from_low, from_high,
    send_c, recv_c, send_y, recv_y, send_r, recv_r, send_l, recv_l,
):
    me = lax.axis_index("beam")
    core = lax.rem(me, 2)
    side = lax.rem(me // 2, 2)
    place = me // 4
    other_core = me + 1 - 2 * core
    other_side = me + 2 - 4 * side
    above = me + 4
    below = me - 4
    first = place == 0
    last = place == deep - 1

    barrier = pltpu.get_barrier_semaphore()
    for there in (other_core, other_side):
        pl.semaphore_signal(barrier, inc=1, device_id={"beam": there}, device_id_type=MESH)

    @pl.when(place > 0)
    def _():
        pl.semaphore_signal(barrier, inc=1, device_id={"beam": below}, device_id_type=MESH)

    @pl.when(place < deep - 1)
    def _():
        pl.semaphore_signal(barrier, inc=1, device_id={"beam": above}, device_id_type=MESH)

    pl.semaphore_wait(barrier, jnp.where(first | last, 3, 4))

    chunk = width // ROUNDS
    tail = fold.shape[2]
    norm = jnp.sum(power_in[...] * power_in[...])
    lane = lax.broadcasted_iota(jnp.int32, (coef.shape[0] // 2, width), 1)

    def copy(source, target, send, recv, there):
        return pltpu.make_async_remote_copy(
            src_ref=source, dst_ref=target, send_sem=send, recv_sem=recv,
            device_id={"beam": there}, device_id_type=MESH,
        )

    def core_copy(k):
        return copy(own.at[k, 1 - core], from_core.at[k], send_c.at[k], recv_c.at[k], other_core)

    def side_copy(k):
        return copy(own.at[k, core, 1 - side], from_y.at[k], send_y.at[k], recv_y.at[k], other_side)

    def up_copy(k, j):
        return copy(
            own.at[k, core, side, j], from_low.at[k, j], send_r.at[k, j], recv_r.at[k, j], above
        )

    def down_copy(k, j):
        return copy(
            own.at[k, core, side, j], from_high.at[k, j], send_l.at[k, j], recv_l.at[k, j], below
        )

    def window_row(i, tile):
        row = i + jnp.where(i < anchors[tile, 0], width, 0)
        values = matrix[row]
        start = values[:tail] * fold[tile, 0] + values[2 * width :] * fold[tile, 1]
        return jnp.concatenate([start, values[tail : 2 * width]], 0)

    def compute(k):
        def body(step, carry):
            waves = []
            for part in range(ROWS):
                i = k * chunk + step * ROWS + part
                right = jnp.concatenate([window_row(i, t) for t in range(TILES)], 1)
                waves.append(
                    lax.dot_general(
                        coef[...], right, (((1,), (1,)), ((), ())),
                        preferred_element_type=jnp.float32,
                    )
                )
            wave = jnp.concatenate(waves, 0)
            high = wave.astype(jnp.bfloat16)
            low = (wave - high.astype(jnp.float32)).astype(jnp.bfloat16)
            full = jnp.dot(high, table[0], preferred_element_type=jnp.float32)
            full += jnp.dot(low, table[0], preferred_element_type=jnp.float32)
            full += jnp.dot(high, table[1], preferred_element_type=jnp.float32)
            count = coef.shape[0] // 2
            shape = own.shape[1:4] + (8, width)
            for part in range(ROWS):
                a = full[2 * part * count : (2 * part + 1) * count]
                b = full[(2 * part + 1) * count : (2 * part + 2) * count]
                real = a[:, :width] - b[:, width:]
                imag = a[:, width:] + b[:, :width]
                real = jnp.where(lane == width // 2, norm, real)
                own[k, :, :, :, step * ROWS + part, 0] = real.reshape(shape)
                own[k, :, :, :, step * ROWS + part, 1] = imag.reshape(shape)
            return carry

        lax.fori_loop(0, chunk // ROWS, body, 0)

    def phase(it, carry):
        @pl.when(it < ROUNDS)
        def _():
            compute(it)
            core_copy(it).start()

        k1 = it - 1

        @pl.when((k1 >= 0) & (k1 < ROUNDS))
        def _():
            core_copy(k1).wait_recv()
            own[k1, core, 1 - side] += from_core[k1, 1 - side]
            side_copy(k1).start()
            own[k1, core, side] += from_core[k1, side]

        k2 = it - 2

        @pl.when((k2 >= 0) & (k2 < ROUNDS))
        def _():
            side_copy(k2).wait_recv()
            own[k2, core, side] += from_y[k2]

        ku = it - 2 - place

        @pl.when((ku >= 0) & (ku < ROUNDS))
        def _():
            for j in range(deep - 1, 0, -1):

                @pl.when(j > place)
                def _():
                    @pl.when(place > 0)
                    def _():
                        up_copy(ku, j).wait_recv()
                        own[ku, core, side, j] += from_low[ku, j]

                    up_copy(ku, j).start()

        kd = it - 2 - (deep - 1 - place)

        @pl.when((kd >= 0) & (kd < ROUNDS))
        def _():
            for j in range(deep - 1):

                @pl.when(j < place)
                def _():
                    @pl.when(place < deep - 1)
                    def _():
                        down_copy(kd, j).wait_recv()
                        own[kd, core, side, j] += from_high[kd, j]

                    down_copy(kd, j).start()

        kf = it - 1 - deep

        @pl.when((kf >= 0) & (kf < ROUNDS))
        def _():
            @pl.when(place > 0)
            def _():
                up_copy(kf, place).wait_recv()
                own[kf, core, side, place] += from_low[kf, place]

            @pl.when(place < deep - 1)
            def _():
                down_copy(kf, place).wait_recv()
                own[kf, core, side, place] += from_high[kf, place]

            out[kf] = own[kf, core, side, place]

        return carry

    lax.fori_loop(0, ROUNDS + deep + 1, phase, 0)

    def drain(k, carry):
        core_copy(k).wait_send()
        side_copy(k).wait_send()
        for j in range(deep):

            @pl.when(j > place)
            def _():
                up_copy(k, j).wait_send()

            @pl.when(j < place)
            def _():
                down_copy(k, j).wait_send()

        return carry

    lax.fori_loop(0, ROUNDS, drain, 0)


def fused(smatrix, amplitude, aberration, beam_list, positions, anchors, masks):
    width = masks.shape[1]
    detectors = masks.shape[0]
    beams = smatrix.shape[3]
    size = lax.axis_size("beam")
    per_device = positions.shape[1] // size
    deep = size // 4
    spots = positions.reshape(-1, 2)
    phase_index = jnp.remainder(
        spots[:, 0:1] * beam_list[None, :, 0] + spots[:, 1:2] * beam_list[None, :, 1], width
    )
    theta = aberration[None, :] - 2.0 * math.pi / width * phase_index.astype(jnp.float32)
    coef = jnp.stack([jnp.cos(theta), jnp.sin(theta)], 0) * amplitude[None, None, :]
    coef = coef.astype(jnp.bfloat16).reshape(2, TILES, deep, 2, 2, per_device, beams)
    coef = coef.transpose(0, 4, 3, 2, 1, 5, 6)[..., None, :]
    same = jnp.eye(TILES, dtype=jnp.bfloat16).reshape(1, 1, 1, 1, TILES, 1, TILES, 1)
    coef = (coef * same).reshape(2 * TILES * positions.shape[1], TILES * beams)
    rows = smatrix.shape[0]
    tail = 2 * (rows - width)
    keep = jnp.arange(tail)[None, :] // 2 >= anchors[:, 1:2]
    fold = jnp.stack([keep, ~keep], 1)[..., None].astype(jnp.bfloat16)
    fold = jnp.broadcast_to(fold, (TILES, 2, tail, beams))
    table = jnp.asarray(column_table(width))
    chunk = width // ROUNDS
    unit = (chunk, 2, 8, width)
    vmem = pl.BlockSpec(memory_space=pltpu.VMEM)
    dma = pltpu.SemaphoreType.DMA
    owned = pl.pallas_call(
        functools.partial(reduce_kernel, deep, width),
        out_shape=jax.ShapeDtypeStruct((ROUNDS,) + unit, jnp.float32),
        in_specs=[pl.BlockSpec(memory_space=pltpu.SMEM)] + [vmem] * 5,
        out_specs=vmem,
        scratch_shapes=[
            pltpu.VMEM((ROUNDS, 2, 2, deep) + unit, jnp.float32),
            pltpu.VMEM((ROUNDS, 2, deep) + unit, jnp.float32),
            pltpu.VMEM((ROUNDS, deep) + unit, jnp.float32),
            pltpu.VMEM((ROUNDS, deep) + unit, jnp.float32),
            pltpu.VMEM((ROUNDS, deep) + unit, jnp.float32),
            dma((ROUNDS,)), dma((ROUNDS,)), dma((ROUNDS,)), dma((ROUNDS,)),
            dma((ROUNDS, deep)), dma((ROUNDS, deep)), dma((ROUNDS, deep)), dma((ROUNDS, deep)),
        ],
        compiler_params=pltpu.CompilerParams(
            collective_id=0, has_side_effects=True, vmem_limit_bytes=60 * 2**20
        ),
    )(
        anchors,
        smatrix.reshape(rows, 2 * smatrix.shape[1], beams),
        coef,
        fold,
        amplitude.reshape(1, beams),
        table,
    )
    owned = owned.reshape(width, 2, 8, width)
    norm = owned[0, 0, 0, width // 2]
    cosine, sine = (jnp.asarray(part, jnp.float32) for part in fourier(width))
    high = lax.Precision.HIGHEST
    rotate = jnp.concatenate([cosine, sine], 0)
    real = jnp.einsum("kr,rul->kul", rotate, owned[:, 0], precision=high)
    imag = jnp.einsum("kr,rul->kul", rotate, owned[:, 1], precision=high)
    full_re = real[:width] + imag[width:]
    full_im = imag[:width] - real[width:]
    power = full_re * full_re + full_im * full_im
    signals = jnp.einsum("kul,dkl->ud", power, masks.astype(jnp.float32), precision=high)
    signals = signals / (norm * width * width)
    return signals.reshape(TILES, per_device, detectors)


def solution(mesh):
    placed = (P(None, None, "parts", "beam"), P("beam"), P("beam"), P("beam", None), P(), P(), P())

    def run(smatrix, amplitude, aberration, beam_list, positions, anchors, masks):
        size = mesh.shape["beam"]
        rows = TILES * positions.shape[1] // size
        inner = fused if size % 4 == 0 and rows == 8 else local
        return jax.shard_map(
            inner, mesh=mesh, in_specs=placed, out_specs=P("parts", "beam", None), check_vma=False
        )(smatrix, amplitude, aberration, beam_list, positions, anchors, masks)

    return run
```

```python
import functools
import math

import jax
import jax.numpy as jnp
import numpy as np
from jax import lax
from jax.experimental import pallas as pl
from jax.experimental.pallas import tpu as pltpu
from jax.sharding import PartitionSpec as P

TILES = 2
ROUNDS = 16
ALONG = 2
LAG = 3
HOP = 2
ROWS = 2
MESH = pl.DeviceIdType.MESH


def coefficients(amplitude, aberration, beam_list, spots, width):
    phase_index = jnp.remainder(
        spots[:, 0:1] * beam_list[None, :, 0] + spots[:, 1:2] * beam_list[None, :, 1], width
    )
    theta = aberration[None, :] - 2.0 * math.pi / width * phase_index.astype(jnp.float32)
    coef_re = (amplitude[None, :] * jnp.cos(theta)).astype(jnp.bfloat16)
    coef_im = (amplitude[None, :] * jnp.sin(theta)).astype(jnp.bfloat16)
    upper = jnp.concatenate([coef_re, -coef_im], 1)
    lower = jnp.concatenate([coef_im, coef_re], 1)
    return jnp.stack([upper, lower], 1)


def window_of(smatrix, corner, width):
    zero = jnp.zeros((), jnp.int32)
    local_beams = smatrix.shape[3]
    window = lax.dynamic_slice(
        smatrix, (corner[0], corner[1], zero, zero), (width, width, 2, local_beams)
    )
    return window.reshape(width * width, 2 * local_beams)


def transform(wave_re, wave_im, width):
    freq = jnp.arange(width, dtype=jnp.int32)
    angle = (
        2.0
        * math.pi
        / width
        * jnp.remainder(freq[:, None] * freq[None, :], width).astype(jnp.float32)
    )
    cosine = jnp.cos(angle)
    sine = jnp.sin(angle)
    high = lax.Precision.HIGHEST
    half_re = jnp.einsum("nrs,sk->nrk", wave_re, cosine, precision=high) + jnp.einsum(
        "nrs,sk->nrk", wave_im, sine, precision=high
    )
    half_im = jnp.einsum("nrs,sk->nrk", wave_im, cosine, precision=high) - jnp.einsum(
        "nrs,sk->nrk", wave_re, sine, precision=high
    )
    full_re = jnp.einsum("jr,nrk->njk", cosine, half_re, precision=high) + jnp.einsum(
        "jr,nrk->njk", sine, half_im, precision=high
    )
    full_im = jnp.einsum("jr,nrk->njk", cosine, half_im, precision=high) - jnp.einsum(
        "jr,nrk->njk", sine, half_re, precision=high
    )
    return (full_re, full_im)


def wave_rows(left, right, count):
    rows = left
    rows = rows.reshape(2 * count, rows.shape[2])
    product = lax.dot_general(
        rows, right, (((1,), (1,)), ((), ())), preferred_element_type=jnp.float32
    )
    product = product.reshape(count, 2, right.shape[0])
    return product


def detect(owned, mask_table, norm, width):
    count = owned.shape[0]
    full_re, full_im = transform(
        owned[:, 0].reshape(count, width, width), owned[:, 1].reshape(count, width, width), width
    )
    power = (full_re * full_re + full_im * full_im).reshape(count, width * width)
    return jnp.einsum("np,dp->nd", power, mask_table, precision=lax.Precision.HIGHEST) / (
        norm * width * width
    )


def local(smatrix, amplitude, aberration, beam_list, positions, anchors, masks):
    width = masks.shape[1]
    detectors = masks.shape[0]
    pixels = width * width
    per_device = positions.shape[1] // lax.axis_size("beam")
    norm = lax.psum(jnp.sum(amplitude * amplitude), "beam")
    mask_table = masks.reshape(detectors, pixels).astype(jnp.float32)
    lefts = []
    rights = []
    for tile in range(TILES):
        lefts.append(coefficients(amplitude, aberration, beam_list, positions[tile], width))
        rights.append(window_of(smatrix, anchors[tile], width))
    outputs = []
    for tile in range(TILES):
        left = lefts[tile]
        right = rights[tile]
        owned = lax.psum_scatter(
            wave_rows(left, right, per_device * lax.axis_size("beam")),
            "beam",
            scatter_dimension=0,
            tiled=True,
        )
        outputs.append(detect(owned, mask_table, norm, width))
    return jnp.stack(outputs, 0)


def fourier(width):
    index = np.arange(width)
    angle = 2.0 * np.pi / width * (np.outer(index, index) % width)
    return np.cos(angle), np.sin(angle)


def halves(table):
    high = table.astype(np.float32).astype(jnp.bfloat16)
    low = (table - high.astype(np.float64)).astype(np.float32).astype(jnp.bfloat16)
    return np.stack([high, low])


def column_table(width):
    cosine, sine = fourier(width)
    table = np.zeros((width, 2, 2, width))
    table[:, 0, 0] = cosine
    table[:, 1, 0] = sine
    table[:, 0, 1] = -sine
    table[:, 1, 1] = cosine
    return halves(table.reshape(2 * width, 2 * width))


def reduce_kernel(
    deep, width, anchors, matrix, coef, fold, power_in, table, out,
    own, from_core, from_y, from_low, from_high, pair_low, pair_high,
    send_c, recv_c, send_y, recv_y, send_r, recv_r, send_l, recv_l,
):
    me = lax.axis_index("beam")
    core = lax.rem(me, 2)
    side = lax.rem(me // 2, 2)
    place = me // 4
    other_core = me + 1 - 2 * core
    other_side = me + 2 - 4 * side
    above = me + 4
    below = me - 4
    first = place == 0
    last = place == deep - 1

    barrier = pltpu.get_barrier_semaphore()
    for there in (other_core, other_side):
        pl.semaphore_signal(barrier, inc=1, device_id={"beam": there}, device_id_type=MESH)

    @pl.when(place > 0)
    def _():
        pl.semaphore_signal(barrier, inc=1, device_id={"beam": below}, device_id_type=MESH)

    @pl.when(place < deep - 1)
    def _():
        pl.semaphore_signal(barrier, inc=1, device_id={"beam": above}, device_id_type=MESH)

    pl.semaphore_wait(barrier, jnp.where(first | last, 3, 4))

    chunk = width // ROUNDS
    tail = fold.shape[2]
    norm = jnp.sum(power_in[...] * power_in[...])
    lane = lax.broadcasted_iota(jnp.int32, (coef.shape[0] // 2, width), 1)

    def copy(source, target, send, recv, there):
        return pltpu.make_async_remote_copy(
            src_ref=source, dst_ref=target, send_sem=send, recv_sem=recv,
            device_id={"beam": there}, device_id_type=MESH,
        )

    def core_copy(k):
        return copy(own.at[k, 1 - core], from_core.at[k], send_c.at[k], recv_c.at[k], other_core)

    def side_copy(k):
        return copy(own.at[k, core, 1 - side], from_y.at[k], send_y.at[k], recv_y.at[k], other_side)

    def up_copy(k, j):
        return copy(
            own.at[k, core, side, j], from_low.at[k, j], send_r.at[k, j], recv_r.at[k, j], above
        )

    def down_copy(k, j):
        return copy(
            own.at[k, core, side, j], from_high.at[k, j], send_l.at[k, j], recv_l.at[k, j], below
        )

    def up_pair(k, j):
        return copy(
            own.at[k, core, :, j], pair_low.at[k // 2, j], send_r.at[k, j], recv_r.at[k, j], above
        )

    def down_pair(k, j):
        return copy(
            own.at[k, core, :, j], pair_high.at[k // 2, j], send_l.at[k, j], recv_l.at[k, j], below
        )

    def last_copy(k):
        return copy(
            own.at[k, core, 1 - side, place], from_y.at[k, 0], send_y.at[k], recv_y.at[k], other_side
        )

    def along(k):
        return (k < 2 * ALONG) & (lax.rem(k, 2) == 1)

    def across(k):
        return (k >= 0) & (k < ROUNDS) & jnp.logical_not(along(k))

    def window_row(i, tile):
        row = i + jnp.where(i < anchors[tile, 0], width, 0)
        values = matrix[row]
        start = values[:tail] * fold[tile, 0] + values[2 * width :] * fold[tile, 1]
        return jnp.concatenate([start, values[tail : 2 * width]], 0)

    def compute(k):
        def body(step, carry):
            waves = []
            for part in range(ROWS):
                i = k * chunk + step * ROWS + part
                right = jnp.concatenate([window_row(i, t) for t in range(TILES)], 1)
                waves.append(
                    lax.dot_general(
                        coef[...], right, (((1,), (1,)), ((), ())),
                        preferred_element_type=jnp.float32,
                    )
                )
            wave = jnp.concatenate(waves, 0)
            high = wave.astype(jnp.bfloat16)
            low = (wave - high.astype(jnp.float32)).astype(jnp.bfloat16)
            full = jnp.dot(high, table[0], preferred_element_type=jnp.float32)
            full += jnp.dot(low, table[0], preferred_element_type=jnp.float32)
            full += jnp.dot(high, table[1], preferred_element_type=jnp.float32)
            count = coef.shape[0] // 2
            shape = own.shape[1:4] + (8, width)
            for part in range(ROWS):
                a = full[2 * part * count : (2 * part + 1) * count]
                b = full[(2 * part + 1) * count : (2 * part + 2) * count]
                real = a[:, :width] - b[:, width:]
                imag = a[:, width:] + b[:, :width]
                real = jnp.where(lane == width // 2, norm, real)
                own[k, :, :, :, step * ROWS + part, 0] = real.reshape(shape)
                own[k, :, :, :, step * ROWS + part, 1] = imag.reshape(shape)
            return carry

        lax.fori_loop(0, chunk // ROWS, body, 0)

    def phase(it, carry):
        @pl.when(it < ROUNDS)
        def _():
            compute(it)
            core_copy(it).start()

        k1 = it - 1

        @pl.when((k1 >= 0) & (k1 < ROUNDS))
        def _():
            core_copy(k1).wait_recv()
            own[k1, core, 1 - side] += from_core[k1, 1 - side]

            @pl.when(across(k1))
            def _():
                side_copy(k1).start()

            own[k1, core, side] += from_core[k1, side]

        def up_step(k, copy_of, held, index):
            for j in range(deep - 1, 0, -1):

                @pl.when(j > place)
                def _():
                    @pl.when(place > 0)
                    def _():
                        copy_of(k, j).wait_recv()
                        own[(k, core) + index + (j,)] += held(k, j)

                    copy_of(k, j).start()

        def down_step(k, copy_of, held, index):
            for j in range(deep - 1):

                @pl.when(j < place)
                def _():
                    @pl.when(place < deep - 1)
                    def _():
                        copy_of(k, j).wait_recv()
                        own[(k, core) + index + (j,)] += held(k, j)

                    copy_of(k, j).start()

        def finish(k, up_of, down_of, low, high, index):
            @pl.when(place > 0)
            def _():
                up_of(k, place).wait_recv()
                own[(k, core) + index + (place,)] += low(k, place)

            @pl.when(place < deep - 1)
            def _():
                down_of(k, place).wait_recv()
                own[(k, core) + index + (place,)] += high(k, place)

        def low_pair(k, j):
            return pair_low[k // 2, j]

        def high_pair(k, j):
            return pair_high[k // 2, j]

        def low_one(k, j):
            return from_low[k, j]

        def high_one(k, j):
            return from_high[k, j]

        both = (slice(None),)
        ku = it - 1 - HOP * place

        @pl.when((ku >= 0) & along(ku))
        def _():
            up_step(ku, up_pair, low_pair, both)

        kd = it - 1 - HOP * (deep - 1 - place)

        @pl.when((kd >= 0) & along(kd))
        def _():
            down_step(kd, down_pair, high_pair, both)

        kf = it - 1 - HOP * (deep - 1)

        @pl.when((kf >= 0) & along(kf))
        def _():
            finish(kf, up_pair, down_pair, low_pair, high_pair, both)
            last_copy(kf).start()

        k2 = it - LAG

        @pl.when(across(k2))
        def _():
            side_copy(k2).wait_recv()
            own[k2, core, side] += from_y[k2]

        one = (side,)
        kv = it - LAG - HOP * place

        @pl.when(across(kv))
        def _():
            up_step(kv, up_copy, low_one, one)

        ke = it - LAG - HOP * (deep - 1 - place)

        @pl.when(across(ke))
        def _():
            down_step(ke, down_copy, high_one, one)

        kg = it - LAG - HOP * (deep - 1)

        @pl.when(across(kg))
        def _():
            finish(kg, up_copy, down_copy, low_one, high_one, one)
            out[kg] = own[kg, core, side, place]

        return carry

    lax.fori_loop(0, ROUNDS + LAG + HOP * (deep - 1), phase, 0)

    def drain(k, carry):
        core_copy(k).wait_send()

        @pl.when(along(k))
        def _():
            last_copy(k).wait()
            out[k] = own[k, core, side, place] + from_y[k, 0]
            for j in range(deep):

                @pl.when(j > place)
                def _():
                    up_pair(k, j).wait_send()

                @pl.when(j < place)
                def _():
                    down_pair(k, j).wait_send()

        @pl.when(across(k))
        def _():
            side_copy(k).wait_send()
            for j in range(deep):

                @pl.when(j > place)
                def _():
                    up_copy(k, j).wait_send()

                @pl.when(j < place)
                def _():
                    down_copy(k, j).wait_send()

        return carry

    lax.fori_loop(0, ROUNDS, drain, 0)


def fused(smatrix, amplitude, aberration, beam_list, positions, anchors, masks):
    width = masks.shape[1]
    detectors = masks.shape[0]
    beams = smatrix.shape[3]
    size = lax.axis_size("beam")
    per_device = positions.shape[1] // size
    deep = size // 4
    spots = positions.reshape(-1, 2)
    phase_index = jnp.remainder(
        spots[:, 0:1] * beam_list[None, :, 0] + spots[:, 1:2] * beam_list[None, :, 1], width
    )
    theta = aberration[None, :] - 2.0 * math.pi / width * phase_index.astype(jnp.float32)
    coef = jnp.stack([jnp.cos(theta), jnp.sin(theta)], 0) * amplitude[None, None, :]
    coef = coef.astype(jnp.bfloat16).reshape(2, TILES, deep, 2, 2, per_device, beams)
    coef = coef.transpose(0, 4, 3, 2, 1, 5, 6)[..., None, :]
    same = jnp.eye(TILES, dtype=jnp.bfloat16).reshape(1, 1, 1, 1, TILES, 1, TILES, 1)
    coef = (coef * same).reshape(2 * TILES * positions.shape[1], TILES * beams)
    rows = smatrix.shape[0]
    tail = 2 * (rows - width)
    keep = jnp.arange(tail)[None, :] // 2 >= anchors[:, 1:2]
    fold = jnp.stack([keep, ~keep], 1)[..., None].astype(jnp.bfloat16)
    fold = jnp.broadcast_to(fold, (TILES, 2, tail, beams))
    table = jnp.asarray(column_table(width))
    chunk = width // ROUNDS
    unit = (chunk, 2, 8, width)
    vmem = pl.BlockSpec(memory_space=pltpu.VMEM)
    dma = pltpu.SemaphoreType.DMA
    owned = pl.pallas_call(
        functools.partial(reduce_kernel, deep, width),
        out_shape=jax.ShapeDtypeStruct((ROUNDS,) + unit, jnp.float32),
        in_specs=[pl.BlockSpec(memory_space=pltpu.SMEM)] + [vmem] * 5,
        out_specs=vmem,
        scratch_shapes=[
            pltpu.VMEM((ROUNDS, 2, 2, deep) + unit, jnp.float32),
            pltpu.VMEM((ROUNDS, 2, deep) + unit, jnp.float32),
            pltpu.VMEM((ROUNDS, deep) + unit, jnp.float32),
            pltpu.VMEM((ROUNDS, deep) + unit, jnp.float32),
            pltpu.VMEM((ROUNDS, deep) + unit, jnp.float32),
            pltpu.VMEM((ALONG, deep, 2) + unit, jnp.float32),
            pltpu.VMEM((ALONG, deep, 2) + unit, jnp.float32),
            dma((ROUNDS,)), dma((ROUNDS,)), dma((ROUNDS,)), dma((ROUNDS,)),
            dma((ROUNDS, deep)), dma((ROUNDS, deep)), dma((ROUNDS, deep)), dma((ROUNDS, deep)),
        ],
        compiler_params=pltpu.CompilerParams(
            collective_id=0, has_side_effects=True, vmem_limit_bytes=60 * 2**20
        ),
    )(
        anchors,
        smatrix.reshape(rows, 2 * smatrix.shape[1], beams),
        coef,
        fold,
        amplitude.reshape(1, beams),
        table,
    )
    owned = owned.reshape(width, 2, 8, width)
    norm = owned[0, 0, 0, width // 2]
    cosine, sine = (jnp.asarray(part, jnp.float32) for part in fourier(width))
    high = lax.Precision.HIGHEST
    rotate = jnp.concatenate([cosine, sine], 0)
    real = jnp.einsum("kr,rul->kul", rotate, owned[:, 0], precision=high)
    imag = jnp.einsum("kr,rul->kul", rotate, owned[:, 1], precision=high)
    full_re = real[:width] + imag[width:]
    full_im = imag[:width] - real[width:]
    power = full_re * full_re + full_im * full_im
    signals = jnp.einsum("kul,dkl->ud", power, masks.astype(jnp.float32), precision=high)
    signals = signals / (norm * width * width)
    return signals.reshape(TILES, per_device, detectors)


def solution(mesh):
    placed = (P(None, None, "parts", "beam"), P("beam"), P("beam"), P("beam", None), P(), P(), P())

    def run(smatrix, amplitude, aberration, beam_list, positions, anchors, masks):
        size = mesh.shape["beam"]
        rows = TILES * positions.shape[1] // size
        inner = fused if size % 4 == 0 and rows == 8 else local
        return jax.shard_map(
            inner, mesh=mesh, in_specs=placed, out_specs=P("parts", "beam", None), check_vma=False
        )(smatrix, amplitude, aberration, beam_list, positions, anchors, masks)

    return run
```
